128 devices in a mesh: section: 8 (over y_lo, z), replica: 16 (over x, y_hi, core).
Axes of the slice: x: 4, y: 4 (y_hi: 2, y_lo: 2; y = y_hi * 2 + y_lo), z: 4, core: 2. Of those that a mesh axis runs over, the one named last changes fastest.
Arguments:
- arriving: bfloat16 [8, 16, 6, 64, 2560], P('section', 'replica'), may hold values from -6 to 6
- stash: bfloat16 [8, 16, 6, 64, 2560], P('section', 'replica'), may hold values from -6 to 6
- cotangent: bfloat16 [8, 16, 6, 64, 2560], P('section', 'replica'), may hold values from -6 to 6
- weight: bfloat16 [8, 16, 2560, 2560], P('section', 'replica'), may hold values from -0.125 to 0.125
- gain: bfloat16 [8, 16, 2560], P('section', 'replica'), may hold values from 0.099609375 to 1.8984375
- routes_fwd: int32 [8, 96, 2], P('section'), may hold values from -1 to 15, as said below
- routes_bwd: int32 [8, 96, 2], P('section'), may hold values from -1 to 15, as said below
- partner: int32 [8, 16], P('section'), may hold values from 0 to 15, as said below
- shard_pick: int32 [8], P('section'), may hold values from 0 to 19
Outputs:
- forward_out: bfloat16 [8, 16, 6, 64, 2560], P('section', 'replica')
- backward_out: bfloat16 [8, 16, 6, 64, 2560], P('section', 'replica')
- averaged: bfloat16 [8, 16, 128, 2560], P('section', 'replica')
The draws below stay inside these ranges and needn't reach their ends.
Inputs may be any that keep to these rules, and one draw needn't show every extreme that they name: `routes_fwd`: in each section group the live entries (both columns >= 0; -1 in both columns marks an unused entry) put at most 6 on one replica of the group and at most 6 on one replica of the neighbouring group, and no pair of replicas is named by two live entries; in every section group some replica holds exactly 6 and some receiving replica gets exactly 6. `routes_bwd`: as for routes_fwd, with the previous section group as neighbour. partner[s, partner[s, r]] = r and partner[s, r] != r.
All inputs are finite; a program needn't handle non-finite values.
Results may differ from the reference program's by a relative error of at most 0.006.
Values may be sent and summed in bfloat16 or wider, within the bound.
A program may use at most 128 MiB of HBM per device.

```python
import jax
import jax.numpy as jnp
from jax import lax

WIDTH = 2560
MB_TOKENS = 64
SLOTS = 6
SHARD_ROWS = 128
SECTIONS = 8
REPLICAS = 16


def edge_routes(key):
    keys = jax.random.split(key, SECTIONS)

    def one_section(section_key):
        parts = jax.random.split(section_key, 5)
        source_perm = jax.random.permutation(parts[0], REPLICAS).astype(jnp.int32)
        target_perm = jax.random.permutation(parts[1], REPLICAS).astype(jnp.int32)
        level = jnp.left_shift(jnp.int32(1), jax.random.randint(parts[2], (REPLICAS,), 0, 4, dtype=jnp.int32))
        level = jnp.minimum(level, SLOTS)
        level = level.at[0].set(SLOTS)
        coin = jax.random.randint(parts[3], (REPLICAS, SLOTS), 0, SLOTS, dtype=jnp.int32)
        rows = jnp.arange(REPLICAS, dtype=jnp.int32)[:, None]
        offsets = jnp.arange(SLOTS, dtype=jnp.int32)[None, :]
        target = (rows + offsets) % REPLICAS
        keep = (coin < level[:, None]) | (target == 0)
        current = jnp.broadcast_to(source_perm[:, None], (REPLICAS, SLOTS))
        following = target_perm[target]
        current = jnp.where(keep, current, -1)
        following = jnp.where(keep, following, -1)
        pairs = jnp.stack([current.reshape(-1), following.reshape(-1)], axis=-1)
        order = jax.random.permutation(parts[4], REPLICAS * SLOTS)
        return pairs[order].astype(jnp.int32)
    return jax.vmap(one_section)(keys)


def draw_routes_fwd(key, part):
    key = jax.random.fold_in(key, 3)
    return edge_routes(key)


def draw_routes_bwd(key, part):
    key = jax.random.fold_in(key, 5)
    return edge_routes(key)


def draw_partner(key, part):
    key = jax.random.fold_in(key, 7)
    keys = jax.random.split(key, SECTIONS)

    def one_section(section_key):
        order = jax.random.permutation(section_key, REPLICAS).astype(jnp.int32)
        evens = order[0::2]
        odds = order[1::2]
        mates = jnp.zeros((REPLICAS,), jnp.int32)
        return mates.at[evens].set(odds).at[odds].set(evens)
    return jax.vmap(one_section)(keys)


def with_ends(values, own_key, low, largest):
    longest = values.shape.index(max(values.shape))
    spots = []
    for shift in (0, 1):
        where = [jax.random.randint(jax.random.fold_in(own_key, axis), (), 0, length) for axis, length in enumerate(values.shape)]
        where[longest] = (where[longest] + shift) % values.shape[longest]
        spots.append(tuple(where))
    return values.at[spots[0]].set(low).at[spots[1]].set(largest)


def level_of(stream_key, dims, pieces, least, top_value):
    level, own = 1.0, jax.random.fold_in(stream_key, 6)
    for position, blocks in pieces:
        steps = jnp.exp(jax.random.uniform(jax.random.fold_in(own, position), (blocks,), jnp.float32, least / len(pieces), top_value / len(pieces)))
        level = level * jnp.repeat(steps, dims[position] // blocks).reshape([-1 if axis == position else 1 for axis in range(len(dims))])
    return level


def noise(key, dims, spread, reach, shards=(), kind=jnp.bfloat16):
    values = spread * jax.random.normal(key, dims, jnp.float32)
    if shards:
        values = values * level_of(key, dims, shards, -0.22, 0.18)
    return jnp.clip(values, -reach, reach).astype(kind)


def setup_inputs(seed: int = 0) -> dict:
    streams_of = jax.random.split(jax.random.key(seed), 10)
    arriving = noise(streams_of[0], (SECTIONS, REPLICAS, SLOTS, MB_TOKENS, WIDTH), 1.0, 6.0, ((0, 8), (1, 16)))
    stash = noise(streams_of[1], (SECTIONS, REPLICAS, SLOTS, MB_TOKENS, WIDTH), 1.0, 6.0, ((0, 8), (1, 16)))
    cotangent = noise(streams_of[2], (SECTIONS, REPLICAS, SLOTS, MB_TOKENS, WIDTH), 1.0, 6.0, ((0, 8), (1, 16)))
    weight = noise(streams_of[3], (SECTIONS, REPLICAS, WIDTH, WIDTH), WIDTH ** -0.5, 0.125, ((0, 8), (1, 16)))
    gain = jnp.clip(1.0 + 0.18 * jax.random.normal(streams_of[4], (SECTIONS, REPLICAS, WIDTH), jnp.float32), 0.099609375, 1.8984375).astype(jnp.bfloat16)
    routes_fwd = draw_routes_fwd(jax.random.fold_in(streams_of[9], 71), 0)
    routes_bwd = draw_routes_bwd(jax.random.fold_in(streams_of[9], 71), 0)
    partner = draw_partner(jax.random.fold_in(streams_of[9], 71), 0)
    shard_pick = with_ends(jax.random.randint(streams_of[8], (SECTIONS,), 0, WIDTH // SHARD_ROWS), jax.random.fold_in(streams_of[8], 1), 0, (WIDTH // SHARD_ROWS) - 1).astype(jnp.int32)
    return dict(arriving=arriving, stash=stash, cotangent=cotangent, weight=weight, gain=gain, routes_fwd=routes_fwd, routes_bwd=routes_bwd, partner=partner, shard_pick=shard_pick)


EPS = 1e-05
LEARN = 0.002

def normalize(inputs, gain_row):
    values = inputs.astype(jnp.float32)
    scale = lax.rsqrt(lax.optimization_barrier(jnp.mean(values * values, axis=-1, keepdims=True)) + EPS)
    return ((values * scale * gain_row.astype(jnp.float32)).astype(jnp.bfloat16), scale)

def slot_ranks(column, count):
    onehot = (column[:, None] == jnp.arange(count, dtype=jnp.int32)[None, :]).astype(jnp.int32)
    before = jnp.cumsum(onehot, axis=0) - onehot
    return lax.optimization_barrier(jnp.sum(before * onehot, axis=1)).astype(jnp.int32)

def forward_work(weights, gain_row, inputs):
    flat_in = inputs.reshape(-1, inputs.shape[-1])
    normed, scale = normalize(flat_in, gain_row)
    pre = jnp.dot(normed, weights, preferred_element_type=jnp.float32)
    result = (flat_in.astype(jnp.float32) + jax.nn.silu(pre)).astype(jnp.bfloat16)
    return result.reshape(inputs.shape)

def backward_work(weights, gain_row, stash_rows, cotan_rows, live, pick, shard_rows):
    width = stash_rows.shape[-1]
    flat_stash = stash_rows.reshape(-1, width)
    normed_b, scale = normalize(flat_stash, gain_row)
    pre_b = jnp.dot(normed_b, weights, preferred_element_type=jnp.float32)
    sigma = jax.nn.sigmoid(pre_b)
    flat_cot = cotan_rows.reshape(-1, width).astype(jnp.float32)
    row_live = jnp.repeat(live, stash_rows.shape[1])[:, None]
    dpre = (flat_cot * sigma * (1.0 + pre_b * (1.0 - sigma)) * row_live).astype(jnp.bfloat16)
    dnorm = lax.dot_general(dpre, weights, (((1,), (1,)), ((), ())), preferred_element_type=jnp.float32)
    weighted = dnorm * gain_row.astype(jnp.float32)
    stash_f = flat_stash.astype(jnp.float32)
    mean_term = lax.optimization_barrier(jnp.mean(weighted * stash_f, axis=-1, keepdims=True))
    input_grad = (flat_cot + scale * (weighted - stash_f * scale * scale * mean_term)).astype(jnp.bfloat16)
    start = (pick * shard_rows).astype(jnp.int32)
    columns = lax.dynamic_slice_in_dim(normed_b, start, shard_rows, 1)
    grad = lax.dot_general(columns, dpre, (((0,), (0,)), ((), ())), preferred_element_type=jnp.float32)
    block = lax.dynamic_slice_in_dim(weights, start, shard_rows, 0)
    updated = (block.astype(jnp.float32) - LEARN * grad).astype(jnp.bfloat16)
    return (input_grad.reshape(stash_rows.shape), updated)

def route_table(pairs, step):
    current = pairs[:, :, 0]
    following = pairs[:, :, 1]
    live = current >= 0
    from_slot = jax.vmap(lambda col: slot_ranks(col, REPLICAS))(current)
    to_slot = jax.vmap(lambda col: slot_ranks(col, REPLICAS))(following)
    section_ids = jnp.arange(SECTIONS, dtype=jnp.int32)[:, None]
    source = (section_ids * REPLICAS + current) * SLOTS + from_slot
    target_section = (section_ids + step) % SECTIONS
    target = (target_section * REPLICAS + following) * SLOTS + to_slot
    total = SECTIONS * REPLICAS * SLOTS
    target = jnp.where(live, target, total).astype(jnp.int32)
    table = jnp.full((total,), -1, dtype=jnp.int32)
    return table.at[target.reshape(-1)].set(source.reshape(-1).astype(jnp.int32), mode='drop')

def place(results, table):
    total = SECTIONS * REPLICAS * SLOTS
    flat = results.reshape(total, MB_TOKENS, WIDTH)
    picked = flat[jnp.clip(table, 0, total - 1)]
    kept = jnp.where((table >= 0)[:, None, None], picked, jnp.zeros_like(picked))
    return kept.reshape(results.shape)

def reference(arriving, stash, cotangent, weight, gain, routes_fwd, routes_bwd, partner, shard_pick):
    current_b = routes_bwd[:, :, 0]
    counts = lax.optimization_barrier(jnp.sum((current_b[:, :, None] == jnp.arange(REPLICAS, dtype=jnp.int32)[None, None, :]).astype(jnp.int32), axis=1))
    live = (jnp.arange(SLOTS, dtype=jnp.int32)[None, None, :] < counts[:, :, None]).astype(jnp.float32)
    devices = SECTIONS * REPLICAS
    picks = jnp.repeat(shard_pick, REPLICAS)

    def one_device(items):
        weights, gain_row, inputs, stash_rows, cotan_rows, live_row, pick = items
        result = forward_work(weights, gain_row, inputs)
        input_grad, updated = backward_work(weights, gain_row, stash_rows, cotan_rows, live_row, pick, SHARD_ROWS)
        return (result, input_grad, updated)
    results, grads, updated = lax.map(one_device, (weight.reshape(devices, WIDTH, WIDTH), gain.reshape(devices, WIDTH), arriving.reshape(devices, SLOTS, MB_TOKENS, WIDTH), stash.reshape(devices, SLOTS, MB_TOKENS, WIDTH), cotangent.reshape(devices, SLOTS, MB_TOKENS, WIDTH), live.reshape(devices, SLOTS), picks))
    forward_out = place(results, route_table(routes_fwd, 1)).reshape(arriving.shape)
    backward_out = place(grads, route_table(routes_bwd, -1)).reshape(arriving.shape)
    updated = updated.reshape(SECTIONS, REPLICAS, SHARD_ROWS, WIDTH)
    mates = updated[jnp.arange(SECTIONS, dtype=jnp.int32)[:, None], partner]
    averaged = ((updated.astype(jnp.float32) + mates.astype(jnp.float32)) * 0.5).astype(jnp.bfloat16)
    return (forward_out, backward_out, averaged)
```

```python
import functools

import jax
import jax.numpy as jnp
from jax import lax
from jax.experimental import pallas as pl
from jax.experimental.pallas import tpu as pltpu
from jax.sharding import PartitionSpec as P

EPS = 1e-05
LEARN = 0.002
SLOTS = 6
TOKENS = 64
WIDTH = 2560
ROWS = SLOTS * TOKENS
SHARD = 128
XS = 4
QUARTER = WIDTH // XS
CHUNKS = 4
PART = TOKENS // CHUNKS
HELD = XS * SLOTS
TILE = 512
TILES = WIDTH // TILE
MESH = pl.DeviceIdType.MESH
BF = jnp.bfloat16
F32 = jnp.float32


def ranks(column):
    order = jnp.arange(column.shape[-1], dtype=jnp.int32)
    same = column[:, :, None] == column[:, None, :]
    before = order[None, None, :] < order[None, :, None]
    return jnp.sum((same & before).astype(jnp.int32), axis=2)


def tables(routes_fwd, routes_bwd, mates, replica):
    h = (replica // 2) % 2
    c = replica % 2
    pairs = jnp.stack([routes_fwd, routes_bwd])
    current, following = pairs[:, :, 0], pairs[:, :, 1]
    place = jnp.where(following >= 0, following * SLOTS + ranks(following), -1)
    held = jnp.where(current % 2 == c, 0, HELD) + (current // 4) * SLOTS + ranks(current)
    near = (current // 2) % 2 == h
    slot = jnp.arange(HELD, dtype=jnp.int32)
    x, t = slot // SLOTS, slot % SLOTS
    stay = ((x * 2 + h) * 2 + c) * SLOTS + t
    leave = ((x * 2 + 1 - h) * 2 + c) * SLOTS + t
    hit_stay = place[:, None, :] == stay[None, :, None]
    hit_leave = place[:, None, :] == leave[None, :, None]
    here = near[:, None, :]
    empty = 2 * HELD
    value = held[:, None, :] - empty
    keep = empty + jnp.sum(jnp.where(hit_stay & here, value, 0), axis=2)
    cross = empty + jnp.sum(jnp.where(hit_leave & here, value, 0), axis=2)
    come = jnp.any(hit_stay & ~here, axis=2)
    keep = jnp.where(come, empty + 1 + slot, keep)
    count = jnp.sum((routes_bwd[:, 0] == replica).astype(jnp.int32))
    column = jnp.arange(XS, dtype=jnp.int32)
    mine = mates[(column * 2 + h) * 2 + c]
    theirs = mates[(column * 2 + 1 - h) * 2 + c]

    def where_held(mate):
        return jnp.where(mate % 2 == c, 0, XS) + mate // 4

    mate_keep = jnp.where((mine // 2) % 2 == h, where_held(mine), 2 * XS + column)
    mate_cross = jnp.where((theirs // 2) % 2 == h, where_held(theirs), 0)
    live = (jnp.arange(SLOTS, dtype=jnp.int32) < count).astype(jnp.float32)
    return (
        jnp.concatenate(
            [cross.reshape(-1), keep.reshape(-1), mate_cross, mate_keep]
        ),
        live,
    )


CROSS, KEEP = 0, 2 * HELD
MATE_CROSS = 4 * HELD
MATE_KEEP = MATE_CROSS + XS


def kernel(table, live, gain, st_cols, gain_cols, w_rows, arr_hbm, st_hbm, ct_hbm, w_hbm, fo, bo, ao, *scratch):
    scratch = list(scratch)

    def take(n):
        out = scratch[:n]
        del scratch[:n]
        return out

    (xf, xb, yb, w, normed, dpre, dnorm, scale, upd, mu, hru, hsu, avu) = take(13)
    items = 2 * CHUNKS
    m, hr, hs, xs = take(items), take(items), take(items), take(items)
    (wsem, insem, x1s, x1r, lsem, cs, cr, hss, hsr, x2s, x2r) = take(11)

    section = lax.axis_index("section")
    replica = lax.axis_index("replica")
    x = replica // 4
    hc = replica % 4
    h, c = hc // 2, hc % 2

    def wcopy(j):
        cols = pl.ds(j * TILE, TILE)
        return pltpu.make_async_copy(w_hbm.at[:, cols], w.at[:, cols], wsem.at[j])

    loads = [
        pltpu.make_async_copy(src, dst, insem.at[i])
        for i, (src, dst) in enumerate(((arr_hbm, xf), (st_hbm, xb), (ct_hbm, yb)))
    ]
    loads[0].start()
    for j in range(TILES):
        wcopy(j).start()
    loads[1].start()
    loads[2].start()

    def at(ds, xx, hh, cc):
        return (lax.rem(section + ds + 8, 8), xx * 4 + hh * 2 + cc)

    xpeers = {d: lax.rem(x + d, XS) for d in (1, 3, 2)}
    hpeer = at(0, x, 1 - h, c)
    cpeer = at(0, x, h, 1 - c)

    barrier = pltpu.get_barrier_semaphore()
    greet = [at(0, xx, h, c) for xx in xpeers.values()] + [hpeer, cpeer]
    for ds in (1, -1):
        greet += [at(ds, xx, h, c) for xx in range(XS)]
    for device in greet:
        pl.semaphore_signal(barrier, inc=1, device_id=device, device_id_type=MESH)

    for i in range(items):
        m[i][2 * HELD] = jnp.zeros((PART, QUARTER), BF)

    def norm(src):
        g = gain[...].astype(F32)

        def block(i, _):
            v = src[i].astype(F32)
            inv = lax.rsqrt(jnp.mean(v * v, axis=-1, keepdims=True) + EPS)
            rows = pl.ds(pl.multiple_of(i * TOKENS, TOKENS), TOKENS)
            normed[rows, :] = (v * inv * g).astype(BF)
            scale[rows, :] = jnp.broadcast_to(inv, (TOKENS, 128))
            return 0

        lax.fori_loop(0, SLOTS, block, 0)

    loads[0].wait()
    norm(xf)
    for j in range(TILES):
        wcopy(j).wait()
        cols = pl.ds(j * TILE, TILE)
        pre = jnp.dot(normed[...], w[:, cols], preferred_element_type=F32)
        v = xf[:, :, cols].reshape(ROWS, TILE).astype(F32)
        out = v + pre / (1.0 + jnp.exp(-pre))
        xf[:, :, cols] = out.astype(BF).reshape(SLOTS, TOKENS, TILE)

    pl.semaphore_wait(barrier, len(greet))

    def remote(src, dst, ssem, rsem, device):
        return pltpu.make_async_remote_copy(
            src_ref=src, dst_ref=dst, send_sem=ssem, recv_sem=rsem, device_id=device, device_id_type=MESH
        )

    sends = []

    def quarter(xx):
        return pl.ds(pl.multiple_of(xx * QUARTER, 128), QUARTER)

    def spread_copies(i):
        src = xf if i < CHUNKS else yb
        rows = pl.ds((i % CHUNKS) * PART, PART)
        out = []
        for n, (d, xx) in enumerate(xpeers.items()):
            out.append(
                remote(
                    src.at[:, rows, quarter(xx)],
                    m[i].at[pl.ds(x * SLOTS, SLOTS)],
                    x1s.at[i, n],
                    x1r.at[i, n],
                    at(0, xx, h, c),
                )
            )
        own = pltpu.make_async_copy(src.at[:, rows, quarter(x)], m[i].at[pl.ds(x * SLOTS, SLOTS)], lsem.at[i])
        return out, own

    def spread(i):
        out, own = spread_copies(i)
        for cp in out:
            cp.start()
            sends.append(cp)
        own.start()

    def mirror_copy(i):
        return remote(m[i].at[pl.ds(0, HELD)], m[i].at[pl.ds(HELD, HELD)], cs.at[i], cr.at[i], cpeer)

    def mirror(i):
        out, own = spread_copies(i)
        for cp in out:
            cp.wait_recv()
        own.wait()
        cp = mirror_copy(i)
        cp.start()
        sends.append(cp)

    def cross_copy(i):
        return remote(hs[i], hr[i], hss.at[i], hsr.at[i], hpeer)

    def cross(i):
        mirror_copy(i).wait_recv()
        base = CROSS + (i // CHUNKS) * HELD

        def one(j, _):
            hs[i][j] = m[i][table[base + j]]
            return 0

        lax.fori_loop(0, HELD, one, 0)
        cp = cross_copy(i)
        cp.start()
        sends.append(cp)

    def deliver_copies(i):
        out = []
        rows = pl.ds((i % CHUNKS) * PART, PART)
        target = fo if i < CHUNKS else bo
        for d in (1, 3, 2, 0):
            xx = lax.rem(x + d, XS)
            out.append(
                remote(
                    xs[i].at[pl.ds(xx * SLOTS, SLOTS)],
                    target.at[:, rows, quarter(x)],
                    x2s.at[i, d],
                    x2r.at[i, d],
                    at(1 if i < CHUNKS else -1, xx, h, c),
                )
            )
        return out

    def deliver(i):
        cross_copy(i).wait_recv()
        base = (i // CHUNKS) * HELD

        def one(j, _):
            xs[i][j] = m[i][table[KEEP + base + j]]
            return 0

        def bring(j, _):
            m[i][2 * HELD + 1 + j] = hr[i][j]
            return 0

        lax.fori_loop(0, HELD, bring, 0)
        lax.fori_loop(0, HELD, one, 0)
        for cp in deliver_copies(i):
            cp.start()
            sends.append(cp)

    u = items

    def spread_u_copies():
        out = []
        for n, (d, xx) in enumerate(xpeers.items()):
            out.append(remote(upd.at[:, quarter(xx)], mu.at[x], x1s.at[u, n], x1r.at[u, n], at(0, xx, h, c)))
        return out, pltpu.make_async_copy(upd.at[:, quarter(x)], mu.at[x], lsem.at[u])

    def spread_u():
        out, own = spread_u_copies()
        for cp in out:
            cp.start()
            sends.append(cp)
        own.start()

    def mirror_u_copy():
        return remote(mu.at[pl.ds(0, XS)], mu.at[pl.ds(XS, XS)], cs.at[u], cr.at[u], cpeer)

    def mirror_u():
        out, own = spread_u_copies()
        for cp in out:
            cp.wait_recv()
        own.wait()
        cp = mirror_u_copy()
        cp.start()
        sends.append(cp)

    def cross_u_copy():
        return remote(hsu, hru, hss.at[u], hsr.at[u], hpeer)

    def cross_u():
        mirror_u_copy().wait_recv()

        def one(j, _):
            hsu[j] = mu[table[MATE_CROSS + j]]
            return 0

        lax.fori_loop(0, XS, one, 0)
        cp = cross_u_copy()
        cp.start()
        sends.append(cp)

    def deliver_u_copies():
        out = []
        for n, (d, xx) in enumerate(xpeers.items()):
            out.append(remote(avu.at[xx], ao.at[:, quarter(x)], x2s.at[u, n], x2r.at[u, n], at(0, xx, h, c)))
        return out, pltpu.make_async_copy(avu.at[x], ao.at[:, quarter(x)], x2r.at[u, 3])

    def deliver_u():
        cross_u_copy().wait_recv()

        def one(j, _):
            mate = mu[table[MATE_KEEP + j]]
            avu[j] = ((mu[j].astype(F32) + mate.astype(F32)) * 0.5).astype(BF)
            return 0

        for j in range(XS):
            mu[2 * XS + j] = hru[j]
        lax.fori_loop(0, XS, one, 0)
        out, own = deliver_u_copies()
        for cp in out:
            cp.start()
            sends.append(cp)
        own.start()

    for i in range(CHUNKS):
        spread(i)

    loads[1].wait()
    loads[2].wait()
    norm(xb)
    for j in range(TILES):
        if j == 2:
            mirror(0)
        if j == 3:
            cross(0)
        if j == 4:
            mirror(1)
        cols = pl.ds(j * TILE, TILE)
        pre = jnp.dot(normed[...], w[:, cols], preferred_element_type=F32)
        sig = 1.0 / (1.0 + jnp.exp(-pre))
        v = yb[:, :, cols].reshape(ROWS, TILE).astype(F32)
        d = v * sig * (1.0 + pre * (1.0 - sig))
        for i in range(SLOTS):
            rows = slice(i * TOKENS, (i + 1) * TOKENS)
            dpre[rows, cols] = (d[rows] * live[i]).astype(BF)
    cross(1)
    picked = st_cols[...].reshape(ROWS, SHARD).astype(F32)
    columns = (picked * scale[...] * gain_cols[...].astype(F32)).astype(BF)
    for j in range(TILES):
        cols = pl.ds(j * TILE, TILE)
        grad = lax.dot_general(columns, dpre[:, cols], (((0,), (0,)), ((), ())), preferred_element_type=F32)
        upd[:, cols] = (w_rows[:, cols].astype(F32) - LEARN * grad).astype(BF)
    spread_u()
    mirror(2)
    cross(2)
    for j in range(TILES):
        if j == 2:
            mirror(3)
        if j == 3:
            cross(3)
        rows = pl.ds(j * TILE, TILE)
        dnorm[:, rows] = lax.dot_general(
            dpre[...], w[rows, :], (((1,), (1,)), ((), ())), preferred_element_type=F32
        )

    def finish(k):
        g = gain[...].astype(F32)

        def block(i, _):
            rows = pl.ds(pl.multiple_of(i * TOKENS + k * PART, PART), PART)
            part = pl.ds(k * PART, PART)
            weighted = dnorm[rows, :] * g
            v = xb[i, part, :].astype(F32)
            inv = scale[rows, 0:1]
            mean = jnp.mean(weighted * v, axis=-1, keepdims=True)
            out = yb[i, part, :].astype(F32) + inv * (weighted - v * inv * inv * mean)
            yb[i, part, :] = out.astype(BF)
            return 0

        lax.fori_loop(0, SLOTS, block, 0)

    for k in range(CHUNKS):
        finish(k)
        spread(CHUNKS + k)

    mirror_u()
    deliver(0)
    cross_u()
    order = list(range(items))
    for k in range(CHUNKS):
        mirror(CHUNKS + k)
        if k + 1 < CHUNKS:
            deliver(k + 1)
        cross(CHUNKS + k)
    deliver_u()
    for k in range(CHUNKS):
        deliver(CHUNKS + k)

    for i in range(items):
        for cp in deliver_copies(i):
            cp.wait_recv()
    out, own = deliver_u_copies()
    for cp in out:
        cp.wait_recv()
    own.wait()
    for cp in sends:
        cp.wait_send()


def body(arriving, stash, cotangent, weight, gain, routes_fwd, routes_bwd, partner, shard_pick):
    replica = lax.axis_index("replica")
    table, live = tables(routes_fwd[0], routes_bwd[0], partner[0], replica)
    items = 2 * CHUNKS
    dma = pltpu.SemaphoreType.DMA
    block = (HELD, PART, QUARTER)
    whole = (SLOTS, TOKENS, WIDTH)
    scratch = [
        pltpu.VMEM(whole, BF),
        pltpu.VMEM(whole, BF),
        pltpu.VMEM(whole, BF),
        pltpu.VMEM((WIDTH, WIDTH), BF),
        pltpu.VMEM((ROWS, WIDTH), BF),
        pltpu.VMEM((ROWS, WIDTH), BF),
        pltpu.VMEM((ROWS, WIDTH), F32),
        pltpu.VMEM((ROWS, 128), F32),
        pltpu.VMEM((SHARD, WIDTH), BF),
        pltpu.VMEM((3 * XS, SHARD, QUARTER), BF),
        pltpu.VMEM((XS, SHARD, QUARTER), BF),
        pltpu.VMEM((XS, SHARD, QUARTER), BF),
        pltpu.VMEM((XS, SHARD, QUARTER), BF),
    ]
    scratch += [pltpu.VMEM((3 * HELD + 1, PART, QUARTER), BF)] * items
    scratch += [pltpu.VMEM(block, BF)] * (3 * items)
    scratch += [
        dma((TILES,)),
        dma((3,)),
        dma((items + 1, 3)),
        dma((items + 1, 3)),
        dma((items + 1,)),
        dma((items + 1,)),
        dma((items + 1,)),
        dma((items + 1,)),
        dma((items + 1,)),
        dma((items + 1, 4)),
        dma((items + 1, 4)),
    ]
    start = shard_pick[0] * SHARD
    st_cols = lax.dynamic_slice_in_dim(stash[0, 0], start, SHARD, 2)
    gain_cols = lax.dynamic_slice_in_dim(gain[0], start, SHARD, 1)
    w_rows = lax.dynamic_slice_in_dim(weight[0, 0], start, SHARD, 0)
    anywhere = pl.BlockSpec(memory_space=pl.ANY)
    forward_out, backward_out, averaged = pl.pallas_call(
        kernel,
        out_shape=[
            jax.ShapeDtypeStruct(whole, BF),
            jax.ShapeDtypeStruct(whole, BF),
            jax.ShapeDtypeStruct((SHARD, WIDTH), BF),
        ],
        in_specs=[
            pl.BlockSpec(memory_space=pltpu.SMEM),
            pl.BlockSpec(memory_space=pltpu.SMEM),
            pl.BlockSpec(memory_space=pltpu.VMEM),
            pl.BlockSpec(memory_space=pltpu.VMEM),
            pl.BlockSpec(memory_space=pltpu.VMEM),
            pl.BlockSpec(memory_space=pltpu.VMEM),
            anywhere,
            anywhere,
            anywhere,
            anywhere,
        ],
        out_specs=[anywhere] * 3,
        scratch_shapes=scratch,
        compiler_params=pltpu.CompilerParams(
            collective_id=0, has_side_effects=True, vmem_limit_bytes=63 * 2**20
        ),
        name="replica_step",
    )(table, live, gain[0], st_cols, gain_cols, w_rows, arriving[0, 0], stash[0, 0], cotangent[0, 0], weight[0, 0])
    return forward_out[None, None], backward_out[None, None], averaged[None, None]


def solution(mesh):
    in_specs = (
        P("section", "replica", None, None, None),
        P("section", "replica", None, None, None),
        P("section", "replica", None, None, None),
        P("section", "replica", None, None),
        P("section", "replica", None),
        P("section", None, None),
        P("section", None, None),
        P("section", None),
        P("section"),
    )
    out_specs = (
        P("section", "replica", None, None, None),
        P("section", "replica", None, None, None),
        P("section", "replica", None, None),
    )
    return jax.shard_map(body, mesh=mesh, in_specs=in_specs, out_specs=out_specs, check_vma=False)
```

```python
import functools

import jax
import jax.numpy as jnp
from jax import lax
from jax.experimental import pallas as pl
from jax.experimental.pallas import tpu as pltpu
from jax.sharding import PartitionSpec as P

EPS = 1e-05
LEARN = 0.002
SLOTS = 6
TOKENS = 64
WIDTH = 2560
ROWS = SLOTS * TOKENS
SHARD = 128
XS = 4
QUARTER = WIDTH // XS
CHUNKS = 4
PART = TOKENS // CHUNKS
HELD = XS * SLOTS
TILE = 512
TILES = WIDTH // TILE
MESH = pl.DeviceIdType.MESH
BF = jnp.bfloat16
F32 = jnp.float32


def as_row(column):
    n = column.shape[0]
    eye = lax.broadcasted_iota(jnp.int32, (n, n), 0) == lax.broadcasted_iota(jnp.int32, (n, n), 1)
    return jnp.sum(jnp.where(eye, column, 0), axis=0, keepdims=True)


def as_column(row):
    n = row.shape[1]
    eye = lax.broadcasted_iota(jnp.int32, (n, n), 0) == lax.broadcasted_iota(jnp.int32, (n, n), 1)
    return jnp.sum(jnp.where(eye, row, 0), axis=1, keepdims=True)


def ranks(column):
    n = column.shape[0]
    earlier = lax.broadcasted_iota(jnp.int32, (n, n), 1) < lax.broadcasted_iota(jnp.int32, (n, n), 0)
    same = (as_row(column) == column) & earlier
    return jnp.sum(jnp.where(same, 1, 0), axis=1, keepdims=True)


def route_rows(pairs, h, c):
    current, following = as_column(pairs[0:1, :]), as_column(pairs[1:2, :])
    place = jnp.where(following >= 0, following * SLOTS + ranks(following), -1)
    held = jnp.where((current & 1) == c, 0, HELD) + (current >> 2) * SLOTS + ranks(current)
    near = ((current >> 1) & 1) == h
    value = jnp.where(near, held - 2 * HELD, 0)
    slot = lax.broadcasted_iota(jnp.int32, (1, 128), 1)
    column = jnp.zeros_like(slot)
    for k in range(1, XS):
        column = column + jnp.where(slot >= k * SLOTS, 1, 0)
    t = slot - column * SLOTS

    def look(hh):
        wanted = jnp.where(slot < HELD, ((column * 2 + hh) * 2 + c) * SLOTS + t, -2)
        index = 2 * HELD + jnp.sum(jnp.where(place == wanted, value, 0), axis=0, keepdims=True)
        return jnp.minimum(jnp.maximum(index, 0), 2 * HELD)

    return look(1 - h), look(h)


def mate_rows(mates, h, c):
    slot = lax.broadcasted_iota(jnp.int32, (1, 128), 1)
    number = lax.broadcasted_iota(jnp.int32, (mates.shape[1], 1), 0)
    column = as_column(mates)

    def mate_of(hh):
        return jnp.sum(jnp.where(number == (slot * 2 + hh) * 2 + c, column, 0), axis=0, keepdims=True)

    def found(mate, otherwise):
        here = jnp.where((mate & 1) == c, 0, XS) + (mate >> 2)
        return jnp.where(((mate >> 1) & 1) == h, here, otherwise)

    return found(mate_of(1 - h), 0), found(mate_of(h), 2 * XS + (slot & 3))


CROSS, KEEP = (0, 2), (1, 3)
MATE_CROSS, MATE_KEEP = 4, 5


def kernel(pick, gain, routes_fwd, routes_bwd, partner, arr_hbm, st_hbm, ct_hbm, w_hbm, fo, bo, ao, *scratch):
    scratch = list(scratch)

    def take(n):
        out = scratch[:n]
        del scratch[:n]
        return out

    (xf, xb, yb, w, normed, dpre, dnorm, scale, upd, mu, hru, hsu, avu, rows_v, table, live) = take(16)
    items = 2 * CHUNKS
    m, hr, hs, ht, hts = take(items), take(items), take(items), take(items), take(items)
    xs = hs
    (wsem, insem, x1s, x1r, lsem, cs, cr, hss, hsr, hts_s, hts_r, x2s, x2r) = take(13)

    section = lax.axis_index("section")
    replica = lax.axis_index("replica")
    x = replica // 4
    hc = replica % 4
    h, c = hc // 2, hc % 2
    y, z = section // 4, section % 4
    turns = (z == 3, z == 0)

    def wcopy(j):
        cols = pl.ds(j * TILE, TILE)
        return pltpu.make_async_copy(w_hbm.at[:, :, cols], w.at[:, :, cols], wsem.at[j])

    loads = [
        pltpu.make_async_copy(src, dst, insem.at[i])
        for i, (src, dst) in enumerate(((arr_hbm, xf), (st_hbm, xb), (ct_hbm, yb)))
    ]
    loads[0].start()
    for j in range(TILES):
        wcopy(j).start()
    loads[1].start()
    loads[2].start()

    def at(xx, hh, cc):
        return (section, xx * 4 + hh * 2 + cc)

    def next_z(k, xx):
        return (y * 4 + lax.rem(z + (1, 3)[k], 4), xx * 4 + h * 2 + c)

    def across(k, hh):
        yy = jnp.where(turns[k], 1 - y, y)
        return (yy * 4 + z, x * 4 + hh * 2 + c)

    xpeers = {d: lax.rem(x + d, XS) for d in (1, 3, 2)}
    hpeer = at(x, 1 - h, c)
    cpeer = at(x, h, 1 - c)

    barrier = pltpu.get_barrier_semaphore()
    greet = [at(xx, h, c) for xx in xpeers.values()] + [hpeer, cpeer]
    for k in (0, 1):
        greet += [next_z(k, xx) for xx in range(XS)]
    greet += [((1 - y) * 4 + z, x * 4 + hh * 2 + c) for hh in (0, 1)]
    for device in greet:
        pl.semaphore_signal(barrier, inc=1, device_id=device, device_id_type=MESH)

    for i in range(items):
        m[i][2 * HELD] = jnp.zeros((PART, QUARTER), BF)

    def norm(src):
        g = gain[...].astype(F32)

        def block(i, _):
            v = src[i].astype(F32)
            inv = lax.rsqrt(jnp.mean(v * v, axis=-1, keepdims=True) + EPS)
            rows = pl.ds(pl.multiple_of(i * TOKENS, TOKENS), TOKENS)
            normed[rows, :] = (v * inv * g).astype(BF)
            scale[rows, :] = jnp.broadcast_to(inv, (TOKENS, 128))
            return 0

        lax.fori_loop(0, SLOTS, block, 0)

    for k, pairs in enumerate((routes_fwd[...], routes_bwd[...])):
        leave, stay = route_rows(pairs, h, c)
        rows_v[CROSS[k] : CROSS[k] + 1, :] = leave
        rows_v[KEEP[k] : KEEP[k] + 1, :] = stay
    leave, stay = mate_rows(partner[...], h, c)
    rows_v[MATE_CROSS : MATE_CROSS + 1, :] = leave
    rows_v[MATE_KEEP : MATE_KEEP + 1, :] = stay
    rows_v[6:8, :] = jnp.zeros((2, 128), jnp.int32)
    to_scalars = pltpu.make_async_copy(rows_v, table, insem.at[3])
    to_scalars.start()
    count = jnp.sum(jnp.where(routes_bwd[0:1, :] == replica, 1, 0), axis=1, keepdims=True)
    live[...] = jnp.where(lax.broadcasted_iota(jnp.int32, (8, 128), 0) < count, 1.0, 0.0)

    loads[0].wait()
    norm(xf)
    for j in range(TILES):
        wcopy(j).wait()
        cols = pl.ds(j * TILE, TILE)
        pre = jnp.dot(normed[...], w[:, :, cols].reshape(WIDTH, TILE), preferred_element_type=F32)
        v = xf[:, :, cols].reshape(ROWS, TILE).astype(F32)
        out = v + pre / (1.0 + jnp.exp(-pre))
        xf[:, :, cols] = out.astype(BF).reshape(SLOTS, TOKENS, TILE)

    pl.semaphore_wait(barrier, len(greet))

    def remote(src, dst, ssem, rsem, device):
        return pltpu.make_async_remote_copy(
            src_ref=src, dst_ref=dst, send_sem=ssem, recv_sem=rsem, device_id=device, device_id_type=MESH
        )

    sends = []

    def quarter(xx):
        return pl.ds(pl.multiple_of(xx * QUARTER, 128), QUARTER)

    def spread_copies(i):
        src = xf if i < CHUNKS else yb
        rows = pl.ds((i % CHUNKS) * PART, PART)
        out = []
        for n, (d, xx) in enumerate(xpeers.items()):
            out.append(
                remote(
                    src.at[:, rows, quarter(xx)],
                    m[i].at[pl.ds(x * SLOTS, SLOTS)],
                    x1s.at[i, n],
                    x1r.at[i, n],
                    at(xx, h, c),
                )
            )
        own = pltpu.make_async_copy(src.at[:, rows, quarter(x)], m[i].at[pl.ds(x * SLOTS, SLOTS)], lsem.at[i])
        return out, own

    def spread(i):
        out, own = spread_copies(i)
        for cp in out:
            cp.start()
            sends.append(cp)
        own.start()

    def mirror_copy(i):
        return remote(m[i].at[pl.ds(0, HELD)], m[i].at[pl.ds(HELD, HELD)], cs.at[i], cr.at[i], cpeer)

    def mirror(i):
        out, own = spread_copies(i)
        for cp in out:
            cp.wait_recv()
        own.wait()
        cp = mirror_copy(i)
        cp.start()
        sends.append(cp)

    def cross_copy(i):
        return remote(hs[i], hr[i], hss.at[i], hsr.at[i], across(i // CHUNKS, 1 - h))

    def turn_copy(i):
        return remote(hts[i], ht[i], hts_s.at[i], hts_r.at[i], across(i // CHUNKS, h))

    def cross(i):
        mirror_copy(i).wait_recv()
        if i == 0:
            to_scalars.wait()
        k = i // CHUNKS

        def pack(target, row):
            def one(j, _):
                target[j] = m[i][table[row, j]]
                return 0

            lax.fori_loop(0, HELD, one, 0)

        pack(hs[i], CROSS[k])
        cross_copy(i).start()

        @pl.when(turns[k])
        def _():
            pack(hts[i], KEEP[k])
            turn_copy(i).start()

        @pl.when(jnp.logical_not(turns[k]))
        def _():
            pack(ht[i], KEEP[k])

    def deliver_copies(i):
        out = []
        rows = pl.ds((i % CHUNKS) * PART, PART)
        target = fo if i < CHUNKS else bo
        for d in (1, 3, 2, 0):
            xx = lax.rem(x + d, XS)
            out.append(
                remote(
                    xs[i].at[pl.ds(xx * SLOTS, SLOTS)],
                    target.at[:, rows, quarter(x)],
                    x2s.at[i, d],
                    x2r.at[i, d],
                    next_z(i // CHUNKS, xx),
                )
            )
        return out

    def deliver(i):
        cross_copy(i).wait_recv()

        @pl.when(turns[i // CHUNKS])
        def _():
            turn_copy(i).wait()

        cross_copy(i).wait_send()

        def one(j, _):
            xs[i][j] = hr[i][j] + ht[i][j]
            return 0

        lax.fori_loop(0, HELD, one, 0)
        for cp in deliver_copies(i):
            cp.start()
            sends.append(cp)

    u = items

    def spread_u_copies():
        out = []
        for n, (d, xx) in enumerate(xpeers.items()):
            out.append(remote(upd.at[:, quarter(xx)], mu.at[x], x1s.at[u, n], x1r.at[u, n], at(xx, h, c)))
        return out, pltpu.make_async_copy(upd.at[:, quarter(x)], mu.at[x], lsem.at[u])

    def spread_u():
        out, own = spread_u_copies()
        for cp in out:
            cp.start()
            sends.append(cp)
        own.start()

    def mirror_u_copy():
        return remote(mu.at[pl.ds(0, XS)], mu.at[pl.ds(XS, XS)], cs.at[u], cr.at[u], cpeer)

    def mirror_u():
        out, own = spread_u_copies()
        for cp in out:
            cp.wait_recv()
        own.wait()
        cp = mirror_u_copy()
        cp.start()
        sends.append(cp)

    def cross_u_copy():
        return remote(hsu, hru, hss.at[u], hsr.at[u], hpeer)

    def cross_u():
        mirror_u_copy().wait_recv()

        def one(j, _):
            hsu[j] = mu[table[MATE_CROSS, j]]
            return 0

        lax.fori_loop(0, XS, one, 0)
        cp = cross_u_copy()
        cp.start()
        sends.append(cp)

    def deliver_u_copies():
        out = []
        for n, (d, xx) in enumerate(xpeers.items()):
            out.append(remote(avu.at[xx], ao.at[:, quarter(x)], x2s.at[u, n], x2r.at[u, n], at(xx, h, c)))
        return out, pltpu.make_async_copy(avu.at[x], ao.at[:, quarter(x)], x2r.at[u, 3])

    def deliver_u():
        cross_u_copy().wait_recv()

        def one(j, _):
            mate = mu[table[MATE_KEEP, j]]
            avu[j] = ((mu[j].astype(F32) + mate.astype(F32)) * 0.5).astype(BF)
            return 0

        for j in range(XS):
            mu[2 * XS + j] = hru[j]
        lax.fori_loop(0, XS, one, 0)
        out, own = deliver_u_copies()
        for cp in out:
            cp.start()
            sends.append(cp)
        own.start()

    for i in range(CHUNKS):
        spread(i)

    loads[1].wait()
    loads[2].wait()
    norm(xb)
    for j in range(TILES):
        if j == 2:
            mirror(0)
        if j == 3:
            cross(0)
        if j == 4:
            mirror(1)
        cols = pl.ds(j * TILE, TILE)
        pre = jnp.dot(normed[...], w[:, :, cols].reshape(WIDTH, TILE), preferred_element_type=F32)
        sig = 1.0 / (1.0 + jnp.exp(-pre))
        v = yb[:, :, cols].reshape(ROWS, TILE).astype(F32)
        d = v * sig * (1.0 + pre * (1.0 - sig))
        for i in range(SLOTS):
            rows = slice(i * TOKENS, (i + 1) * TOKENS)
            dpre[rows, cols] = (d[rows] * live[i : i + 1, 0:1]).astype(BF)
    cross(1)
    feature = lax.broadcasted_iota(jnp.int32, (WIDTH, SHARD), 0)
    wanted = lax.broadcasted_iota(jnp.int32, (WIDTH, SHARD), 1) + pick[0] * SHARD
    select = jnp.where(feature == wanted, 1.0, 0.0).astype(BF)
    columns = jnp.dot(normed[...], select, preferred_element_type=F32).astype(BF)
    for j in range(TILES):
        cols = pl.ds(j * TILE, TILE)
        grad = lax.dot_general(columns, dpre[:, cols], (((0,), (0,)), ((), ())), preferred_element_type=F32)
        upd[:, cols] = (w[pick[0], :, cols].astype(F32) - LEARN * grad).astype(BF)
    spread_u()
    mirror(2)
    cross(2)
    for j in range(TILES):
        if j == 2:
            mirror(3)
        if j == 3:
            cross(3)
        rows = pl.ds(j * TILE, TILE)
        dnorm[:, rows] = lax.dot_general(
            dpre[...], w[4 * j : 4 * j + 4].reshape(TILE, WIDTH), (((1,), (1,)), ((), ())), preferred_element_type=F32
        )

    def finish(k):
        g = gain[...].astype(F32)

        def block(i, _):
            rows = pl.ds(pl.multiple_of(i * TOKENS + k * PART, PART), PART)
            part = pl.ds(k * PART, PART)
            weighted = dnorm[rows, :] * g
            v = xb[i, part, :].astype(F32)
            inv = scale[rows, 0:1]
            mean = jnp.mean(weighted * v, axis=-1, keepdims=True)
            out = yb[i, part, :].astype(F32) + inv * (weighted - v * inv * inv * mean)
            yb[i, part, :] = out.astype(BF)
            return 0

        lax.fori_loop(0, SLOTS, block, 0)

    for k in range(CHUNKS):
        finish(k)
        spread(CHUNKS + k)

    mirror_u()
    deliver(0)
    cross_u()
    order = list(range(items))
    for k in range(CHUNKS):
        mirror(CHUNKS + k)
        if k + 1 < CHUNKS:
            deliver(k + 1)
        cross(CHUNKS + k)
    deliver_u()
    for k in range(CHUNKS):
        deliver(CHUNKS + k)

    for i in range(items):
        for cp in deliver_copies(i):
            cp.wait_recv()
    out, own = deliver_u_copies()
    for cp in out:
        cp.wait_recv()
    own.wait()
    for cp in sends:
        cp.wait_send()


def hand_on(a, b, c, x, y, z, held, rows, into, out):
    ways = [(a.at[i], held.at[i], x.at[i]) for i in range(SLOTS)]
    ways += [(b.at[i], held.at[SLOTS + i], y.at[i]) for i in range(SLOTS)]
    ways += [(c, rows, z)]
    reads = [pltpu.make_async_copy(src, mid, into.at[i]) for i, (src, mid, _) in enumerate(ways)]
    writes = [pltpu.make_async_copy(mid, dst, out.at[i]) for i, (_, mid, dst) in enumerate(ways)]
    for read in reads:
        read.start()
    for read, write in zip(reads, writes):
        read.wait()
        write.start()
    for write in writes:
        write.wait()


def body(arriving, stash, cotangent, weight, gain, routes_fwd, routes_bwd, partner, shard_pick):
    items = 2 * CHUNKS
    dma = pltpu.SemaphoreType.DMA
    block = (HELD, PART, QUARTER)
    whole = (SLOTS, TOKENS, WIDTH)
    scratch = [
        pltpu.VMEM(whole, BF),
        pltpu.VMEM(whole, BF),
        pltpu.VMEM(whole, BF),
        pltpu.VMEM((WIDTH // SHARD, SHARD, WIDTH), BF),
        pltpu.VMEM((ROWS, WIDTH), BF),
        pltpu.VMEM((ROWS, WIDTH), BF),
        pltpu.VMEM((ROWS, WIDTH), F32),
        pltpu.VMEM((ROWS, 128), F32),
        pltpu.VMEM((SHARD, WIDTH), BF),
        pltpu.VMEM((3 * XS, SHARD, QUARTER), BF),
        pltpu.VMEM((XS, SHARD, QUARTER), BF),
        pltpu.VMEM((XS, SHARD, QUARTER), BF),
        pltpu.VMEM((XS, SHARD, QUARTER), BF),
        pltpu.VMEM((8, 128), jnp.int32),
        pltpu.SMEM((8, 128), jnp.int32),
        pltpu.VMEM((8, 128), F32),
    ]
    scratch += [pltpu.VMEM((2 * HELD + 1, PART, QUARTER), BF)] * items
    scratch += [pltpu.VMEM(block, BF)] * (4 * items)
    scratch += [
        dma((TILES,)),
        dma((4,)),
        dma((items + 1, 3)),
        dma((items + 1, 3)),
        dma((items + 1,)),
        dma((items + 1,)),
        dma((items + 1,)),
        dma((items + 1,)),
        dma((items + 1,)),
        dma((items + 1,)),
        dma((items + 1,)),
        dma((items + 1, 4)),
        dma((items + 1, 4)),
    ]
    anywhere = pl.BlockSpec(memory_space=pl.ANY)
    forward_out, backward_out, averaged = pl.pallas_call(
        kernel,
        out_shape=[
            jax.ShapeDtypeStruct(whole, BF),
            jax.ShapeDtypeStruct(whole, BF),
            jax.ShapeDtypeStruct((SHARD, WIDTH), BF),
        ],
        in_specs=[
            pl.BlockSpec(memory_space=pltpu.SMEM),
            pl.BlockSpec(memory_space=pltpu.VMEM),
            pl.BlockSpec(memory_space=pltpu.VMEM),
            pl.BlockSpec(memory_space=pltpu.VMEM),
            pl.BlockSpec(memory_space=pltpu.VMEM),
            anywhere,
            anywhere,
            anywhere,
            anywhere,
        ],
        out_specs=[anywhere] * 3,
        scratch_shapes=scratch,
        compiler_params=pltpu.CompilerParams(
            collective_id=0, has_side_effects=True, vmem_limit_bytes=63 * 2**20
        ),
        name="replica_step",
    )(
        shard_pick,
        gain[0],
        jnp.swapaxes(routes_fwd[0], 0, 1),
        jnp.swapaxes(routes_bwd[0], 0, 1),
        partner,
        arriving[0, 0],
        stash[0, 0],
        cotangent[0, 0],
        weight.reshape(WIDTH // SHARD, SHARD, WIDTH),
    )
    forward_out, backward_out, averaged = pl.pallas_call(
        hand_on,
        out_shape=[
            jax.ShapeDtypeStruct(whole, BF),
            jax.ShapeDtypeStruct(whole, BF),
            jax.ShapeDtypeStruct((SHARD, WIDTH), BF),
        ],
        in_specs=[anywhere] * 3,
        out_specs=[anywhere] * 3,
        scratch_shapes=[
            pltpu.VMEM((2 * SLOTS, TOKENS, WIDTH), BF),
            pltpu.VMEM((SHARD, WIDTH), BF),
            dma((2 * SLOTS + 1,)),
            dma((2 * SLOTS + 1,)),
        ],
        compiler_params=pltpu.CompilerParams(vmem_limit_bytes=63 * 2**20),
        name="hand_on",
    )(forward_out, backward_out, averaged)
    return forward_out[None, None], backward_out[None, None], averaged[None, None]


def solution(mesh):
    in_specs = (
        P("section", "replica", None, None, None),
        P("section", "replica", None, None, None),
        P("section", "replica", None, None, None),
        P("section", "replica", None, None),
        P("section", "replica", None),
        P("section", None, None),
        P("section", None, None),
        P("section", None),
        P("section"),
    )
    out_specs = (
        P("section", "replica", None, None, None),
        P("section", "replica", None, None, None),
        P("section", "replica", None, None),
    )
    return jax.shard_map(body, mesh=mesh, in_specs=in_specs, out_specs=out_specs, check_vma=False)
```

```python
import functools

import jax
import jax.numpy as jnp
from jax import lax
from jax.experimental import pallas as pl
from jax.experimental.pallas import tpu as pltpu
from jax.sharding import PartitionSpec as P

EPS = 1e-05
LEARN = 0.002
SLOTS = 6
TOKENS = 64
WIDTH = 2560
ROWS = SLOTS * TOKENS
HALF = ROWS // 2
SHARD = 128
XS = 4
QUARTER = WIDTH // XS
CHUNKS = 4
PART = TOKENS // CHUNKS
HELD = XS * SLOTS
TILE = 512
TILES = WIDTH // TILE
MESH = pl.DeviceIdType.MESH
BF = jnp.bfloat16
F32 = jnp.float32


def as_row(column):
    n = column.shape[0]
    eye = lax.broadcasted_iota(jnp.int32, (n, n), 0) == lax.broadcasted_iota(jnp.int32, (n, n), 1)
    return jnp.sum(jnp.where(eye, column, 0), axis=0, keepdims=True)


def as_column(row):
    n = row.shape[1]
    eye = lax.broadcasted_iota(jnp.int32, (n, n), 0) == lax.broadcasted_iota(jnp.int32, (n, n), 1)
    return jnp.sum(jnp.where(eye, row, 0), axis=1, keepdims=True)


def ranks(column):
    n = column.shape[0]
    earlier = lax.broadcasted_iota(jnp.int32, (n, n), 1) < lax.broadcasted_iota(jnp.int32, (n, n), 0)
    same = (as_row(column) == column) & earlier
    return jnp.sum(jnp.where(same, 1, 0), axis=1, keepdims=True)


def route_rows(pairs, h, c):
    current, following = as_column(pairs[0:1, :]), as_column(pairs[1:2, :])
    place = jnp.where(following >= 0, following * SLOTS + ranks(following), -1)
    held = jnp.where((current & 1) == c, 0, HELD) + (current >> 2) * SLOTS + ranks(current)
    near = ((current >> 1) & 1) == h
    value = jnp.where(near, held - 2 * HELD, 0)
    slot = lax.broadcasted_iota(jnp.int32, (1, 128), 1)
    column = jnp.zeros_like(slot)
    for k in range(1, XS):
        column = column + jnp.where(slot >= k * SLOTS, 1, 0)
    t = slot - column * SLOTS

    def look(hh):
        wanted = jnp.where(slot < HELD, ((column * 2 + hh) * 2 + c) * SLOTS + t, -2)
        index = 2 * HELD + jnp.sum(jnp.where(place == wanted, value, 0), axis=0, keepdims=True)
        return jnp.minimum(jnp.maximum(index, 0), 2 * HELD)

    return look(1 - h), look(h)


def mate_rows(mates, h, c):
    slot = lax.broadcasted_iota(jnp.int32, (1, 128), 1)
    number = lax.broadcasted_iota(jnp.int32, (mates.shape[1], 1), 0)
    column = as_column(mates)

    def mate_of(hh):
        return jnp.sum(jnp.where(number == (slot * 2 + hh) * 2 + c, column, 0), axis=0, keepdims=True)

    def found(mate, otherwise):
        here = jnp.where((mate & 1) == c, 0, XS) + (mate >> 2)
        return jnp.where(((mate >> 1) & 1) == h, here, otherwise)

    return found(mate_of(1 - h), 0), found(mate_of(h), 2 * XS + (slot & 3))


CROSS, KEEP = (0, 2), (1, 3)
MATE_CROSS, MATE_KEEP = 4, 5


def kernel(pick, gain, routes_fwd, routes_bwd, partner, arr_hbm, st_hbm, ct_hbm, w_hbm, fo, bo, ao, *scratch):
    scratch = list(scratch)

    def take(n):
        out = scratch[:n]
        del scratch[:n]
        return out

    (xf, xb, yb, w, normed, dpre, dnorm, scale, upd, mu, hru, hsu, avu, rows_v, table, live) = take(16)
    items = 2 * CHUNKS
    m, hr, hs, ht, hts = take(items), take(items), take(items), take(items), take(items)
    xs = hs
    (wsem, insem, x1s, x1r, lsem, cs, cr, hss, hsr, hts_s, hts_r, x2s, x2r) = take(13)

    section = lax.axis_index("section")
    replica = lax.axis_index("replica")
    x = replica // 4
    hc = replica % 4
    h, c = hc // 2, hc % 2
    y, z = section // 4, section % 4
    turns = (z == 3, z == 0)

    def wcopy(j):
        cols = pl.ds(j * TILE, TILE)
        return pltpu.make_async_copy(w_hbm.at[:, :, cols], w.at[:, :, cols], wsem.at[j])

    loads = [
        pltpu.make_async_copy(src, dst, insem.at[i])
        for i, (src, dst) in enumerate(((arr_hbm, xf), (st_hbm, xb), (ct_hbm, yb)))
    ]
    loads[0].start()
    for j in range(TILES):
        wcopy(j).start()
    loads[1].start()
    loads[2].start()

    def at(xx, hh, cc):
        return (section, xx * 4 + hh * 2 + cc)

    def next_z(k, xx):
        return (y * 4 + lax.rem(z + (1, 3)[k], 4), xx * 4 + h * 2 + c)

    def across(k, hh):
        yy = jnp.where(turns[k], 1 - y, y)
        return (yy * 4 + z, x * 4 + hh * 2 + c)

    xpeers = {d: lax.rem(x + d, XS) for d in (1, 3, 2)}
    hpeer = at(x, 1 - h, c)
    cpeer = at(x, h, 1 - c)

    barrier = pltpu.get_barrier_semaphore()
    greet = [at(xx, h, c) for xx in xpeers.values()] + [hpeer, cpeer]
    for k in (0, 1):
        greet += [next_z(k, xx) for xx in range(XS)]
    greet += [((1 - y) * 4 + z, x * 4 + hh * 2 + c) for hh in (0, 1)]
    for device in greet:
        pl.semaphore_signal(barrier, inc=1, device_id=device, device_id_type=MESH)

    for i in range(items):
        m[i][2 * HELD] = jnp.zeros((PART, QUARTER), BF)

    def norm_halves(src):
        g = gain[...].astype(F32)

        def block(i, _):
            v = src[i].astype(F32)
            inv = lax.rsqrt(jnp.mean(v * v, axis=-1, keepdims=True) + EPS)
            out = (v * inv * g).astype(BF)
            for half in range(2):
                rows = pl.ds(pl.multiple_of(half * HALF + i * (TOKENS // 2), TOKENS // 2), TOKENS // 2)
                normed[rows, :] = out[half * (TOKENS // 2) : (half + 1) * (TOKENS // 2)]
            return 0

        lax.fori_loop(0, SLOTS, block, 0)

    def norm(src):
        g = gain[...].astype(F32)

        def block(i, _):
            v = src[i].astype(F32)
            inv = lax.rsqrt(jnp.mean(v * v, axis=-1, keepdims=True) + EPS)
            rows = pl.ds(pl.multiple_of(i * TOKENS, TOKENS), TOKENS)
            normed[rows, :] = (v * inv * g).astype(BF)
            scale[rows, :] = jnp.broadcast_to(inv, (TOKENS, 128))
            return 0

        lax.fori_loop(0, SLOTS, block, 0)

    for k, pairs in enumerate((routes_fwd[...], routes_bwd[...])):
        leave, stay = route_rows(pairs, h, c)
        rows_v[CROSS[k] : CROSS[k] + 1, :] = leave
        rows_v[KEEP[k] : KEEP[k] + 1, :] = stay
    leave, stay = mate_rows(partner[...], h, c)
    rows_v[MATE_CROSS : MATE_CROSS + 1, :] = leave
    rows_v[MATE_KEEP : MATE_KEEP + 1, :] = stay
    rows_v[6:8, :] = jnp.zeros((2, 128), jnp.int32)
    to_scalars = pltpu.make_async_copy(rows_v, table, insem.at[3])
    to_scalars.start()
    count = jnp.sum(jnp.where(routes_bwd[0:1, :] == replica, 1, 0), axis=1, keepdims=True)
    live[...] = jnp.where(lax.broadcasted_iota(jnp.int32, (8, 128), 0) < count, 1.0, 0.0)

    loads[0].wait()
    norm_halves(xf)

    def forward(half):
        tokens = pl.ds(half * (TOKENS // 2), TOKENS // 2)
        for j in range(TILES):
            if half == 0:
                wcopy(j).wait()
            cols = pl.ds(j * TILE, TILE)
            pre = jnp.dot(
                normed[half * HALF : (half + 1) * HALF, :],
                w[:, :, cols].reshape(WIDTH, TILE),
                preferred_element_type=F32,
            )
            v = xf[:, tokens, cols].reshape(HALF, TILE).astype(F32)
            out = v + pre / (1.0 + jnp.exp(-pre))
            xf[:, tokens, cols] = out.astype(BF).reshape(SLOTS, TOKENS // 2, TILE)

    forward(0)
    pl.semaphore_wait(barrier, len(greet))

    def remote(src, dst, ssem, rsem, device):
        return pltpu.make_async_remote_copy(
            src_ref=src, dst_ref=dst, send_sem=ssem, recv_sem=rsem, device_id=device, device_id_type=MESH
        )

    sends = []

    def quarter(xx):
        return pl.ds(pl.multiple_of(xx * QUARTER, 128), QUARTER)

    def spread_copies(i):
        src = xf if i < CHUNKS else yb
        rows = pl.ds((i % CHUNKS) * PART, PART)
        out = []
        for n, (d, xx) in enumerate(xpeers.items()):
            out.append(
                remote(
                    src.at[:, rows, quarter(xx)],
                    m[i].at[pl.ds(x * SLOTS, SLOTS)],
                    x1s.at[i, n],
                    x1r.at[i, n],
                    at(xx, h, c),
                )
            )
        own = pltpu.make_async_copy(src.at[:, rows, quarter(x)], m[i].at[pl.ds(x * SLOTS, SLOTS)], lsem.at[i])
        return out, own

    def spread(i):
        out, own = spread_copies(i)
        for cp in out:
            cp.start()
            sends.append(cp)
        own.start()

    def mirror_copy(i):
        return remote(m[i].at[pl.ds(0, HELD)], m[i].at[pl.ds(HELD, HELD)], cs.at[i], cr.at[i], cpeer)

    def mirror(i):
        out, own = spread_copies(i)
        for cp in out:
            cp.wait_recv()
        own.wait()
        cp = mirror_copy(i)
        cp.start()
        sends.append(cp)

    def part_of(p):
        return pl.ds(p * (HELD // 2), HELD // 2)

    def cross_copy(i, p):
        return remote(
            hs[i].at[part_of(p)], hr[i].at[part_of(p)], hss.at[i, p], hsr.at[i, p], across(i // CHUNKS, 1 - h)
        )

    def turn_copy(i, p):
        return remote(
            hts[i].at[part_of(p)], ht[i].at[part_of(p)], hts_s.at[i, p], hts_r.at[i, p], across(i // CHUNKS, h)
        )

    def cross(i):
        mirror_copy(i).wait_recv()
        if i == 0:
            to_scalars.wait()
        k = i // CHUNKS

        def pack(target, row, p):
            def one(j, _):
                target[j] = m[i][table[row, j]]
                return 0

            lax.fori_loop(p * (HELD // 2), (p + 1) * (HELD // 2), one, 0)

        for p in range(2):
            pack(hs[i], CROSS[k], p)
            cross_copy(i, p).start()

            @pl.when(turns[k])
            def _():
                pack(hts[i], KEEP[k], p)
                turn_copy(i, p).start()

        @pl.when(jnp.logical_not(turns[k]))
        def _():
            pack(ht[i], KEEP[k], 0)
            pack(ht[i], KEEP[k], 1)

    def deliver_copy(i, xx):
        target = fo if i < CHUNKS else bo
        rows = pl.ds((i % CHUNKS) * PART, PART)
        return remote(
            xs[i].at[pl.ds(xx * SLOTS, SLOTS)],
            target.at[:, rows, quarter(x)],
            x2s.at[i, xx],
            x2r.at[i, x],
            next_z(i // CHUNKS, xx),
        )

    def delivered(i, xx):
        target = fo if i < CHUNKS else bo
        rows = pl.ds((i % CHUNKS) * PART, PART)
        remote(
            xs[i].at[pl.ds(xx * SLOTS, SLOTS)],
            target.at[:, rows, quarter(xx)],
            x2s.at[i, xx],
            x2r.at[i, xx],
            next_z(i // CHUNKS, xx),
        ).wait_recv()

    def deliver(i):
        for p in range(2):
            cross_copy(i, p).wait_recv()

            @pl.when(turns[i // CHUNKS])
            def _():
                turn_copy(i, p).wait()

            cross_copy(i, p).wait_send()

            def one(j, _):
                xs[i][j] = hr[i][j] + ht[i][j]
                return 0

            lax.fori_loop(p * (HELD // 2), (p + 1) * (HELD // 2), one, 0)
            for xx in (2 * p, 2 * p + 1):
                cp = deliver_copy(i, xx)
                cp.start()
                sends.append(cp)

    u = items

    def spread_u_copies():
        out = []
        for n, (d, xx) in enumerate(xpeers.items()):
            out.append(remote(upd.at[:, quarter(xx)], mu.at[x], x1s.at[u, n], x1r.at[u, n], at(xx, h, c)))
        return out, pltpu.make_async_copy(upd.at[:, quarter(x)], mu.at[x], lsem.at[u])

    def spread_u():
        out, own = spread_u_copies()
        for cp in out:
            cp.start()
            sends.append(cp)
        own.start()

    def mirror_u_copy():
        return remote(mu.at[pl.ds(0, XS)], mu.at[pl.ds(XS, XS)], cs.at[u], cr.at[u], cpeer)

    def mirror_u():
        out, own = spread_u_copies()
        for cp in out:
            cp.wait_recv()
        own.wait()
        cp = mirror_u_copy()
        cp.start()
        sends.append(cp)

    def cross_u_copy():
        return remote(hsu, hru, hss.at[u, 0], hsr.at[u, 0], hpeer)

    def cross_u():
        mirror_u_copy().wait_recv()

        def one(j, _):
            hsu[j] = mu[table[MATE_CROSS, j]]
            return 0

        lax.fori_loop(0, XS, one, 0)
        cp = cross_u_copy()
        cp.start()
        sends.append(cp)

    def deliver_u_copies():
        out = []
        for n, (d, xx) in enumerate(xpeers.items()):
            out.append(remote(avu.at[xx], ao.at[:, quarter(x)], x2s.at[u, n], x2r.at[u, n], at(xx, h, c)))
        return out, pltpu.make_async_copy(avu.at[x], ao.at[:, quarter(x)], x2r.at[u, 3])

    def deliver_u():
        cross_u_copy().wait_recv()

        def one(j, _):
            mate = mu[table[MATE_KEEP, j]]
            avu[j] = ((mu[j].astype(F32) + mate.astype(F32)) * 0.5).astype(BF)
            return 0

        for j in range(XS):
            mu[2 * XS + j] = hru[j]
        lax.fori_loop(0, XS, one, 0)
        out, own = deliver_u_copies()
        for cp in out:
            cp.start()
            sends.append(cp)
        own.start()

    spread(0)
    spread(1)
    forward(1)
    spread(2)
    spread(3)

    loads[1].wait()
    loads[2].wait()
    norm(xb)
    for j in range(TILES):
        if j == 1:
            mirror(0)
        if j == 2:
            cross(0)
        if j == 3:
            mirror(1)
        if j == 4:
            cross(1)
        cols = pl.ds(j * TILE, TILE)
        pre = jnp.dot(normed[...], w[:, :, cols].reshape(WIDTH, TILE), preferred_element_type=F32)
        sig = 1.0 / (1.0 + jnp.exp(-pre))
        v = yb[:, :, cols].reshape(ROWS, TILE).astype(F32)
        d = v * sig * (1.0 + pre * (1.0 - sig))
        for i in range(SLOTS):
            rows = slice(i * TOKENS, (i + 1) * TOKENS)
            dpre[rows, cols] = (d[rows] * live[i : i + 1, 0:1]).astype(BF)
    mirror(2)
    feature = lax.broadcasted_iota(jnp.int32, (WIDTH, SHARD), 0)
    wanted = lax.broadcasted_iota(jnp.int32, (WIDTH, SHARD), 1) + pick[0] * SHARD
    select = jnp.where(feature == wanted, 1.0, 0.0).astype(BF)
    columns = jnp.dot(normed[...], select, preferred_element_type=F32).astype(BF)
    for j in range(TILES):
        cols = pl.ds(j * TILE, TILE)
        grad = lax.dot_general(columns, dpre[:, cols], (((0,), (0,)), ((), ())), preferred_element_type=F32)
        upd[:, cols] = (w[pick[0], :, cols].astype(F32) - LEARN * grad).astype(BF)
    spread_u()
    for j in range(TILES):
        if j == 1:
            deliver(0)
            cross(2)
        if j == 3:
            mirror(3)
        rows = pl.ds(j * TILE, TILE)
        dnorm[:, rows] = lax.dot_general(
            dpre[...], w[4 * j : 4 * j + 4].reshape(TILE, WIDTH), (((1,), (1,)), ((), ())), preferred_element_type=F32
        )

    def finish(k):
        g = gain[...].astype(F32)

        def block(i, _):
            rows = pl.ds(pl.multiple_of(i * TOKENS + k * PART, PART), PART)
            part = pl.ds(k * PART, PART)
            weighted = dnorm[rows, :] * g
            v = xb[i, part, :].astype(F32)
            inv = scale[rows, 0:1]
            mean = jnp.mean(weighted * v, axis=-1, keepdims=True)
            out = yb[i, part, :].astype(F32) + inv * (weighted - v * inv * inv * mean)
            yb[i, part, :] = out.astype(BF)
            return 0

        lax.fori_loop(0, SLOTS, block, 0)

    for k in range(CHUNKS):
        finish(k)
        spread(CHUNKS + k)

    deliver(1)
    cross(3)
    mirror_u()
    deliver(2)
    cross_u()
    mirror(4)
    deliver(3)
    cross(4)
    mirror(5)
    deliver_u()
    cross(5)
    mirror(6)
    deliver(4)
    cross(6)
    mirror(7)
    deliver(5)
    cross(7)
    deliver(6)
    deliver(7)

    for i in range(items):
        for xx in range(XS):
            delivered(i, xx)
    out, own = deliver_u_copies()
    for cp in out:
        cp.wait_recv()
    own.wait()
    for cp in sends:
        cp.wait_send()


def hand_on(a, b, c, x, y, z, held, rows, into, out):
    ways = [(a.at[i], held.at[i], x.at[i]) for i in range(SLOTS)]
    ways += [(b.at[i], held.at[SLOTS + i], y.at[i]) for i in range(SLOTS)]
    ways += [(c, rows, z)]
    reads = [pltpu.make_async_copy(src, mid, into.at[i]) for i, (src, mid, _) in enumerate(ways)]
    writes = [pltpu.make_async_copy(mid, dst, out.at[i]) for i, (_, mid, dst) in enumerate(ways)]
    for read in reads:
        read.start()
    for read, write in zip(reads, writes):
        read.wait()
        write.start()
    for write in writes:
        write.wait()


def body(arriving, stash, cotangent, weight, gain, routes_fwd, routes_bwd, partner, shard_pick):
    items = 2 * CHUNKS
    dma = pltpu.SemaphoreType.DMA
    block = (HELD, PART, QUARTER)
    whole = (SLOTS, TOKENS, WIDTH)
    scratch = [
        pltpu.VMEM(whole, BF),
        pltpu.VMEM(whole, BF),
        pltpu.VMEM(whole, BF),
        pltpu.VMEM((WIDTH // SHARD, SHARD, WIDTH), BF),
        pltpu.VMEM((ROWS, WIDTH), BF),
        pltpu.VMEM((ROWS, WIDTH), BF),
        pltpu.VMEM((ROWS, WIDTH), F32),
        pltpu.VMEM((ROWS, 128), F32),
        pltpu.VMEM((SHARD, WIDTH), BF),
        pltpu.VMEM((3 * XS, SHARD, QUARTER), BF),
        pltpu.VMEM((XS, SHARD, QUARTER), BF),
        pltpu.VMEM((XS, SHARD, QUARTER), BF),
        pltpu.VMEM((XS, SHARD, QUARTER), BF),
        pltpu.VMEM((8, 128), jnp.int32),
        pltpu.SMEM((8, 128), jnp.int32),
        pltpu.VMEM((8, 128), F32),
    ]
    scratch += [pltpu.VMEM((2 * HELD + 1, PART, QUARTER), BF)] * items
    scratch += [pltpu.VMEM(block, BF)] * (4 * items)
    scratch += [
        dma((TILES,)),
        dma((4,)),
        dma((items + 1, 3)),
        dma((items + 1, 3)),
        dma((items + 1,)),
        dma((items + 1,)),
        dma((items + 1,)),
        dma((items + 1, 2)),
        dma((items + 1, 2)),
        dma((items + 1, 2)),
        dma((items + 1, 2)),
        dma((items + 1, 4)),
        dma((items + 1, 4)),
    ]
    anywhere = pl.BlockSpec(memory_space=pl.ANY)
    forward_out, backward_out, averaged = pl.pallas_call(
        kernel,
        out_shape=[
            jax.ShapeDtypeStruct(whole, BF),
            jax.ShapeDtypeStruct(whole, BF),
            jax.ShapeDtypeStruct((SHARD, WIDTH), BF),
        ],
        in_specs=[
            pl.BlockSpec(memory_space=pltpu.SMEM),
            pl.BlockSpec(memory_space=pltpu.VMEM),
            pl.BlockSpec(memory_space=pltpu.VMEM),
            pl.BlockSpec(memory_space=pltpu.VMEM),
            pl.BlockSpec(memory_space=pltpu.VMEM),
            anywhere,
            anywhere,
            anywhere,
            anywhere,
        ],
        out_specs=[anywhere] * 3,
        scratch_shapes=scratch,
        compiler_params=pltpu.CompilerParams(
            collective_id=0, has_side_effects=True, vmem_limit_bytes=63 * 2**20
        ),
        name="replica_step",
    )(
        shard_pick,
        gain[0],
        jnp.swapaxes(routes_fwd[0], 0, 1),
        jnp.swapaxes(routes_bwd[0], 0, 1),
        partner,
        arriving[0, 0],
        stash[0, 0],
        cotangent[0, 0],
        weight.reshape(WIDTH // SHARD, SHARD, WIDTH),
    )
    forward_out, backward_out, averaged = pl.pallas_call(
        hand_on,
        out_shape=[
            jax.ShapeDtypeStruct(whole, BF),
            jax.ShapeDtypeStruct(whole, BF),
            jax.ShapeDtypeStruct((SHARD, WIDTH), BF),
        ],
        in_specs=[anywhere] * 3,
        out_specs=[anywhere] * 3,
        scratch_shapes=[
            pltpu.VMEM((2 * SLOTS, TOKENS, WIDTH), BF),
            pltpu.VMEM((SHARD, WIDTH), BF),
            dma((2 * SLOTS + 1,)),
            dma((2 * SLOTS + 1,)),
        ],
        compiler_params=pltpu.CompilerParams(vmem_limit_bytes=63 * 2**20),
        name="hand_on",
    )(forward_out, backward_out, averaged)
    return forward_out[None, None], backward_out[None, None], averaged[None, None]


def solution(mesh):
    in_specs = (
        P("section", "replica", None, None, None),
        P("section", "replica", None, None, None),
        P("section", "replica", None, None, None),
        P("section", "replica", None, None),
        P("section", "replica", None),
        P("section", None, None),
        P("section", None, None),
        P("section", None),
        P("section"),
    )
    out_specs = (
        P("section", "replica", None, None, None),
        P("section", "replica", None, None, None),
        P("section", "replica", None, None),
    )
    return jax.shard_map(body, mesh=mesh, in_specs=in_specs, out_specs=out_specs, check_vma=False)
```

```python
import functools

import jax
import jax.numpy as jnp
from jax import lax
from jax.experimental import pallas as pl
from jax.experimental.pallas import tpu as pltpu
from jax.sharding import PartitionSpec as P

EPS = 1e-05
LEARN = 0.002
SLOTS = 6
TOKENS = 64
WIDTH = 2560
ROWS = SLOTS * TOKENS
HALF = ROWS // 2
SHARD = 128
XS = 4
QUARTER = WIDTH // XS
CHUNKS = 4
PART = TOKENS // CHUNKS
HELD = XS * SLOTS
TILE = 512
TILES = WIDTH // TILE
STEPS = (1, 3, 2, 0)
MESH = pl.DeviceIdType.MESH
BF = jnp.bfloat16
F32 = jnp.float32


def as_row(column):
    n = column.shape[0]
    eye = lax.broadcasted_iota(jnp.int32, (n, n), 0) == lax.broadcasted_iota(jnp.int32, (n, n), 1)
    return jnp.sum(jnp.where(eye, column, 0), axis=0, keepdims=True)


def as_column(row):
    n = row.shape[1]
    eye = lax.broadcasted_iota(jnp.int32, (n, n), 0) == lax.broadcasted_iota(jnp.int32, (n, n), 1)
    return jnp.sum(jnp.where(eye, row, 0), axis=1, keepdims=True)


def ranks(column):
    n = column.shape[0]
    earlier = lax.broadcasted_iota(jnp.int32, (n, n), 1) < lax.broadcasted_iota(jnp.int32, (n, n), 0)
    same = (as_row(column) == column) & earlier
    return jnp.sum(jnp.where(same, 1, 0), axis=1, keepdims=True)


def route_rows(pairs, h, c):
    current, following = as_column(pairs[0:1, :]), as_column(pairs[1:2, :])
    place = jnp.where(following >= 0, following * SLOTS + ranks(following), -1)
    held = jnp.where((current & 1) == c, 0, HELD) + (current >> 2) * SLOTS + ranks(current)
    near = ((current >> 1) & 1) == h
    value = jnp.where(near, held - 2 * HELD, 0)
    slot = lax.broadcasted_iota(jnp.int32, (1, 128), 1)
    column = jnp.zeros_like(slot)
    for k in range(1, XS):
        column = column + jnp.where(slot >= k * SLOTS, 1, 0)
    t = slot - column * SLOTS

    def look(hh):
        wanted = jnp.where(slot < HELD, ((column * 2 + hh) * 2 + c) * SLOTS + t, -2)
        index = 2 * HELD + jnp.sum(jnp.where(place == wanted, value, 0), axis=0, keepdims=True)
        return jnp.minimum(jnp.maximum(index, 0), 2 * HELD)

    return look(1 - h), look(h)


def mate_rows(mates, h, c):
    slot = lax.broadcasted_iota(jnp.int32, (1, 128), 1)
    number = lax.broadcasted_iota(jnp.int32, (mates.shape[1], 1), 0)
    column = as_column(mates)

    def mate_of(hh):
        return jnp.sum(jnp.where(number == (slot * 2 + hh) * 2 + c, column, 0), axis=0, keepdims=True)

    def found(mate, otherwise):
        here = jnp.where((mate & 1) == c, 0, XS) + (mate >> 2)
        return jnp.where(((mate >> 1) & 1) == h, here, otherwise)

    return found(mate_of(1 - h), 0), found(mate_of(h), 2 * XS + (slot & 3))


CROSS, KEEP = (0, 2), (1, 3)
MATE_CROSS, MATE_KEEP = 4, 5


def kernel(pick, gain, routes_fwd, routes_bwd, partner, arr_hbm, st_hbm, ct_hbm, w_hbm, fo, bo, ao, *scratch):
    scratch = list(scratch)

    def take(n):
        out = scratch[:n]
        del scratch[:n]
        return out

    (xf, xb, yb, w, normed, dpre, dnorm, scale, upd, mu, hru, hsu, avu, rows_v, table, live) = take(16)
    items = 2 * CHUNKS
    m, hr, hs, ht, hts = take(items), take(items), take(items), take(items), take(items)
    xs = hs
    (wsem, insem, x1s, x1r, lsem, cs, cr, hss, hsr, hts_s, hts_r, x2s, x2r) = take(13)

    section = lax.axis_index("section")
    replica = lax.axis_index("replica")
    x = replica // 4
    hc = replica % 4
    h, c = hc // 2, hc % 2
    y, z = section // 4, section % 4
    turns = (z == 3, z == 0)

    def wcopy(j):
        cols = pl.ds(j * TILE, TILE)
        return pltpu.make_async_copy(w_hbm.at[:, :, cols], w.at[:, :, cols], wsem.at[j])

    loads = [
        pltpu.make_async_copy(src, dst, insem.at[i])
        for i, (src, dst) in enumerate(((arr_hbm, xf), (st_hbm, xb), (ct_hbm, yb)))
    ]
    loads[0].start()
    for j in range(TILES):
        wcopy(j).start()
    loads[1].start()
    loads[2].start()

    def at(xx, hh, cc):
        return (section, xx * 4 + hh * 2 + cc)

    def next_z(k, xx):
        return (y * 4 + lax.rem(z + (1, 3)[k], 4), xx * 4 + h * 2 + c)

    def across(k, hh):
        yy = jnp.where(turns[k], 1 - y, y)
        return (yy * 4 + z, x * 4 + hh * 2 + c)

    places = [lax.rem(x + d, XS) for d in STEPS]
    xpeers = dict(zip(STEPS[:3], places))
    hpeer = at(x, 1 - h, c)
    cpeer = at(x, h, 1 - c)

    barrier = pltpu.get_barrier_semaphore()
    greet = [at(xx, h, c) for xx in xpeers.values()] + [hpeer, cpeer]
    for k in (0, 1):
        greet += [next_z(k, xx) for xx in range(XS)]
    greet += [((1 - y) * 4 + z, x * 4 + hh * 2 + c) for hh in (0, 1)]
    for device in greet:
        pl.semaphore_signal(barrier, inc=1, device_id=device, device_id_type=MESH)

    for i in range(items):
        m[i][2 * HELD] = jnp.zeros((PART, QUARTER), BF)

    def norm_halves(src):
        g = gain[...].astype(F32)

        def block(i, _):
            v = src[i].astype(F32)
            inv = lax.rsqrt(jnp.mean(v * v, axis=-1, keepdims=True) + EPS)
            out = (v * inv * g).astype(BF)
            for half in range(2):
                rows = pl.ds(pl.multiple_of(half * HALF + i * (TOKENS // 2), TOKENS // 2), TOKENS // 2)
                normed[rows, :] = out[half * (TOKENS // 2) : (half + 1) * (TOKENS // 2)]
            return 0

        lax.fori_loop(0, SLOTS, block, 0)

    def norm(src):
        g = gain[...].astype(F32)

        def block(i, _):
            v = src[i].astype(F32)
            inv = lax.rsqrt(jnp.mean(v * v, axis=-1, keepdims=True) + EPS)
            rows = pl.ds(pl.multiple_of(i * TOKENS, TOKENS), TOKENS)
            normed[rows, :] = (v * inv * g).astype(BF)
            scale[rows, :] = jnp.broadcast_to(inv, (TOKENS, 128))
            return 0

        lax.fori_loop(0, SLOTS, block, 0)

    for k, pairs in enumerate((routes_fwd[...], routes_bwd[...])):
        leave, stay = route_rows(pairs, h, c)
        rows_v[CROSS[k] : CROSS[k] + 1, :] = leave
        rows_v[KEEP[k] : KEEP[k] + 1, :] = stay
    leave, stay = mate_rows(partner[...], h, c)
    rows_v[MATE_CROSS : MATE_CROSS + 1, :] = leave
    rows_v[MATE_KEEP : MATE_KEEP + 1, :] = stay
    rows_v[6:8, :] = jnp.zeros((2, 128), jnp.int32)
    to_scalars = pltpu.make_async_copy(rows_v, table, insem.at[3])
    to_scalars.start()
    count = jnp.sum(jnp.where(routes_bwd[0:1, :] == replica, 1, 0), axis=1, keepdims=True)
    live[...] = jnp.where(lax.broadcasted_iota(jnp.int32, (8, 128), 0) < count, 1.0, 0.0)

    loads[0].wait()
    norm_halves(xf)

    def forward(half):
        tokens = pl.ds(half * (TOKENS // 2), TOKENS // 2)
        for j in range(TILES):
            if half == 0:
                wcopy(j).wait()
            cols = pl.ds(j * TILE, TILE)
            pre = jnp.dot(
                normed[half * HALF : (half + 1) * HALF, :],
                w[:, :, cols].reshape(WIDTH, TILE),
                preferred_element_type=F32,
            )
            v = xf[:, tokens, cols].reshape(HALF, TILE).astype(F32)
            out = v + pre / (1.0 + jnp.exp(-pre))
            xf[:, tokens, cols] = out.astype(BF).reshape(SLOTS, TOKENS // 2, TILE)

    forward(0)
    pl.semaphore_wait(barrier, len(greet))

    def remote(src, dst, ssem, rsem, device):
        return pltpu.make_async_remote_copy(
            src_ref=src, dst_ref=dst, send_sem=ssem, recv_sem=rsem, device_id=device, device_id_type=MESH
        )

    sends = []

    def quarter(xx):
        return pl.ds(pl.multiple_of(xx * QUARTER, 128), QUARTER)

    def spread_copies(i):
        src = xf if i < CHUNKS else yb
        rows = pl.ds((i % CHUNKS) * PART, PART)
        out = []
        for n, (d, xx) in enumerate(xpeers.items()):
            out.append(
                remote(
                    src.at[:, rows, quarter(xx)],
                    m[i].at[pl.ds(x * SLOTS, SLOTS)],
                    x1s.at[i, n],
                    x1r.at[i, n],
                    at(xx, h, c),
                )
            )
        own = pltpu.make_async_copy(src.at[:, rows, quarter(x)], m[i].at[pl.ds(x * SLOTS, SLOTS)], lsem.at[i])
        return out, own

    def spread(i):
        out, own = spread_copies(i)
        for cp in out:
            cp.start()
            sends.append(cp)
        own.start()

    def mirror_copy(i):
        return remote(m[i].at[pl.ds(0, HELD)], m[i].at[pl.ds(HELD, HELD)], cs.at[i], cr.at[i], cpeer)

    def mirror(i):
        out, own = spread_copies(i)
        for cp in out:
            cp.wait_recv()
        own.wait()
        cp = mirror_copy(i)
        cp.start()
        sends.append(cp)

    def part_of(p):
        return pl.ds(p * (HELD // 2), HELD // 2)

    def cross_copy(i, p):
        return remote(
            hs[i].at[part_of(p)], hr[i].at[part_of(p)], hss.at[i, p], hsr.at[i, p], across(i // CHUNKS, 1 - h)
        )

    def turn_copy(i, p):
        return remote(
            hts[i].at[part_of(p)], ht[i].at[part_of(p)], hts_s.at[i, p], hts_r.at[i, p], across(i // CHUNKS, h)
        )

    def cross(i):
        mirror_copy(i).wait_recv()
        if i == 0:
            to_scalars.wait()
        k = i // CHUNKS

        def pack(target, row, p):
            for q in (2 * p, 2 * p + 1):

                def one(j, _):
                    target[q * SLOTS + j] = m[i][table[row, places[q] * SLOTS + j]]
                    return 0

                lax.fori_loop(0, SLOTS, one, 0)

        for p in range(2):
            pack(hs[i], CROSS[k], p)
            cross_copy(i, p).start()

            @pl.when(turns[k])
            def _():
                pack(hts[i], KEEP[k], p)
                turn_copy(i, p).start()

        @pl.when(jnp.logical_not(turns[k]))
        def _():
            pack(ht[i], KEEP[k], 0)
            pack(ht[i], KEEP[k], 1)

    def deliver_copy(i, q, source):
        target = fo if i < CHUNKS else bo
        rows = pl.ds((i % CHUNKS) * PART, PART)
        return remote(
            xs[i].at[pl.ds(q * SLOTS, SLOTS)],
            target.at[:, rows, quarter(source)],
            x2s.at[i, q],
            x2r.at[i, q],
            next_z(i // CHUNKS, places[q]),
        )

    def deliver(i):
        for p in range(2):
            cross_copy(i, p).wait_recv()

            @pl.when(turns[i // CHUNKS])
            def _():
                turn_copy(i, p).wait()

            cross_copy(i, p).wait_send()

            def one(j, _):
                xs[i][j] = hr[i][j] + ht[i][j]
                return 0

            lax.fori_loop(p * (HELD // 2), (p + 1) * (HELD // 2), one, 0)
            for q in (2 * p, 2 * p + 1):
                cp = deliver_copy(i, q, x)
                cp.start()
                sends.append(cp)

    u = items

    def spread_u_copies():
        out = []
        for n, (d, xx) in enumerate(xpeers.items()):
            out.append(remote(upd.at[:, quarter(xx)], mu.at[x], x1s.at[u, n], x1r.at[u, n], at(xx, h, c)))
        return out, pltpu.make_async_copy(upd.at[:, quarter(x)], mu.at[x], lsem.at[u])

    def spread_u():
        out, own = spread_u_copies()
        for cp in out:
            cp.start()
            sends.append(cp)
        own.start()

    def mirror_u_copy():
        return remote(mu.at[pl.ds(0, XS)], mu.at[pl.ds(XS, XS)], cs.at[u], cr.at[u], cpeer)

    def mirror_u():
        out, own = spread_u_copies()
        for cp in out:
            cp.wait_recv()
        own.wait()
        cp = mirror_u_copy()
        cp.start()
        sends.append(cp)

    def cross_u_copy():
        return remote(hsu, hru, hss.at[u, 0], hsr.at[u, 0], hpeer)

    def cross_u():
        mirror_u_copy().wait_recv()

        def one(j, _):
            hsu[j] = mu[table[MATE_CROSS, j]]
            return 0

        lax.fori_loop(0, XS, one, 0)
        cp = cross_u_copy()
        cp.start()
        sends.append(cp)

    def deliver_u_copies():
        out = []
        for n, (d, xx) in enumerate(xpeers.items()):
            out.append(remote(avu.at[xx], ao.at[:, quarter(x)], x2s.at[u, n], x2r.at[u, n], at(xx, h, c)))
        return out, pltpu.make_async_copy(avu.at[x], ao.at[:, quarter(x)], x2r.at[u, 3])

    def deliver_u():
        cross_u_copy().wait_recv()

        def one(j, _):
            mate = mu[table[MATE_KEEP, j]]
            avu[j] = ((mu[j].astype(F32) + mate.astype(F32)) * 0.5).astype(BF)
            return 0

        for j in range(XS):
            mu[2 * XS + j] = hru[j]
        lax.fori_loop(0, XS, one, 0)
        out, own = deliver_u_copies()
        for cp in out:
            cp.start()
            sends.append(cp)
        own.start()

    spread(0)
    spread(1)
    forward(1)
    spread(2)
    spread(3)

    loads[1].wait()
    loads[2].wait()
    norm(xb)
    for j in range(TILES):
        if j == 1:
            mirror(0)
        if j == 2:
            cross(0)
        if j == 3:
            mirror(1)
        if j == 4:
            cross(1)
        cols = pl.ds(j * TILE, TILE)
        pre = jnp.dot(normed[...], w[:, :, cols].reshape(WIDTH, TILE), preferred_element_type=F32)
        sig = 1.0 / (1.0 + jnp.exp(-pre))
        v = yb[:, :, cols].reshape(ROWS, TILE).astype(F32)
        d = v * sig * (1.0 + pre * (1.0 - sig))
        for i in range(SLOTS):
            rows = slice(i * TOKENS, (i + 1) * TOKENS)
            dpre[rows, cols] = (d[rows] * live[i : i + 1, 0:1]).astype(BF)
    mirror(2)
    feature = lax.broadcasted_iota(jnp.int32, (WIDTH, SHARD), 0)
    wanted = lax.broadcasted_iota(jnp.int32, (WIDTH, SHARD), 1) + pick[0] * SHARD
    select = jnp.where(feature == wanted, 1.0, 0.0).astype(BF)
    columns = jnp.dot(normed[...], select, preferred_element_type=F32).astype(BF)
    for j in range(TILES):
        cols = pl.ds(j * TILE, TILE)
        grad = lax.dot_general(columns, dpre[:, cols], (((0,), (0,)), ((), ())), preferred_element_type=F32)
        upd[:, cols] = (w[pick[0], :, cols].astype(F32) - LEARN * grad).astype(BF)
    spread_u()
    for j in range(TILES):
        if j == 1:
            deliver(0)
            cross(2)
        if j == 3:
            mirror(3)
        rows = pl.ds(j * TILE, TILE)
        dnorm[:, rows] = lax.dot_general(
            dpre[...], w[4 * j : 4 * j + 4].reshape(TILE, WIDTH), (((1,), (1,)), ((), ())), preferred_element_type=F32
        )

    def finish(k):
        g = gain[...].astype(F32)

        def block(i, _):
            rows = pl.ds(pl.multiple_of(i * TOKENS + k * PART, PART), PART)
            part = pl.ds(k * PART, PART)
            weighted = dnorm[rows, :] * g
            v = xb[i, part, :].astype(F32)
            inv = scale[rows, 0:1]
            mean = jnp.mean(weighted * v, axis=-1, keepdims=True)
            out = yb[i, part, :].astype(F32) + inv * (weighted - v * inv * inv * mean)
            yb[i, part, :] = out.astype(BF)
            return 0

        lax.fori_loop(0, SLOTS, block, 0)

    for k in range(CHUNKS):
        finish(k)
        spread(CHUNKS + k)

    deliver(1)
    cross(3)
    mirror(4)
    deliver(2)
    cross(4)
    mirror_u()
    mirror(5)
    deliver(3)
    cross_u()
    deliver(4)
    cross(5)
    mirror(6)
    deliver_u()
    cross(6)
    mirror(7)
    deliver(5)
    cross(7)
    deliver(6)
    deliver(7)

    for i in range(items):
        for q in range(XS):
            deliver_copy(i, q, lax.rem(x - STEPS[q] + XS, XS)).wait_recv()
    out, own = deliver_u_copies()
    for cp in out:
        cp.wait_recv()
    own.wait()
    for cp in sends:
        cp.wait_send()


def hand_on(a, b, c, x, y, z, held, rows, into, out):
    ways = [(a.at[i], held.at[i], x.at[i]) for i in range(SLOTS)]
    ways += [(b.at[i], held.at[SLOTS + i], y.at[i]) for i in range(SLOTS)]
    ways += [(c, rows, z)]
    reads = [pltpu.make_async_copy(src, mid, into.at[i]) for i, (src, mid, _) in enumerate(ways)]
    writes = [pltpu.make_async_copy(mid, dst, out.at[i]) for i, (_, mid, dst) in enumerate(ways)]
    for read in reads:
        read.start()
    for read, write in zip(reads, writes):
        read.wait()
        write.start()
    for write in writes:
        write.wait()


def body(arriving, stash, cotangent, weight, gain, routes_fwd, routes_bwd, partner, shard_pick):
    items = 2 * CHUNKS
    dma = pltpu.SemaphoreType.DMA
    block = (HELD, PART, QUARTER)
    whole = (SLOTS, TOKENS, WIDTH)
    scratch = [
        pltpu.VMEM(whole, BF),
        pltpu.VMEM(whole, BF),
        pltpu.VMEM(whole, BF),
        pltpu.VMEM((WIDTH // SHARD, SHARD, WIDTH), BF),
        pltpu.VMEM((ROWS, WIDTH), BF),
        pltpu.VMEM((ROWS, WIDTH), BF),
        pltpu.VMEM((ROWS, WIDTH), F32),
        pltpu.VMEM((ROWS, 128), F32),
        pltpu.VMEM((SHARD, WIDTH), BF),
        pltpu.VMEM((3 * XS, SHARD, QUARTER), BF),
        pltpu.VMEM((XS, SHARD, QUARTER), BF),
        pltpu.VMEM((XS, SHARD, QUARTER), BF),
        pltpu.VMEM((XS, SHARD, QUARTER), BF),
        pltpu.VMEM((8, 128), jnp.int32),
        pltpu.SMEM((8, 128), jnp.int32),
        pltpu.VMEM((8, 128), F32),
    ]
    scratch += [pltpu.VMEM((2 * HELD + 1, PART, QUARTER), BF)] * items
    scratch += [pltpu.VMEM(block, BF)] * (4 * items)
    scratch += [
        dma((TILES,)),
        dma((4,)),
        dma((items + 1, 3)),
        dma((items + 1, 3)),
        dma((items + 1,)),
        dma((items + 1,)),
        dma((items + 1,)),
        dma((items + 1, 2)),
        dma((items + 1, 2)),
        dma((items + 1, 2)),
        dma((items + 1, 2)),
        dma((items + 1, 4)),
        dma((items + 1, 4)),
    ]
    anywhere = pl.BlockSpec(memory_space=pl.ANY)
    forward_out, backward_out, averaged = pl.pallas_call(
        kernel,
        out_shape=[
            jax.ShapeDtypeStruct(whole, BF),
            jax.ShapeDtypeStruct(whole, BF),
            jax.ShapeDtypeStruct((SHARD, WIDTH), BF),
        ],
        in_specs=[
            pl.BlockSpec(memory_space=pltpu.SMEM),
            pl.BlockSpec(memory_space=pltpu.VMEM),
            pl.BlockSpec(memory_space=pltpu.VMEM),
            pl.BlockSpec(memory_space=pltpu.VMEM),
            pl.BlockSpec(memory_space=pltpu.VMEM),
            anywhere,
            anywhere,
            anywhere,
            anywhere,
        ],
        out_specs=[anywhere] * 3,
        scratch_shapes=scratch,
        compiler_params=pltpu.CompilerParams(
            collective_id=0, has_side_effects=True, vmem_limit_bytes=63 * 2**20
        ),
        name="replica_step",
    )(
        shard_pick,
        gain[0],
        jnp.swapaxes(routes_fwd[0], 0, 1),
        jnp.swapaxes(routes_bwd[0], 0, 1),
        partner,
        arriving[0, 0],
        stash[0, 0],
        cotangent[0, 0],
        weight.reshape(WIDTH // SHARD, SHARD, WIDTH),
    )
    forward_out, backward_out, averaged = pl.pallas_call(
        hand_on,
        out_shape=[
            jax.ShapeDtypeStruct(whole, BF),
            jax.ShapeDtypeStruct(whole, BF),
            jax.ShapeDtypeStruct((SHARD, WIDTH), BF),
        ],
        in_specs=[anywhere] * 3,
        out_specs=[anywhere] * 3,
        scratch_shapes=[
            pltpu.VMEM((2 * SLOTS, TOKENS, WIDTH), BF),
            pltpu.VMEM((SHARD, WIDTH), BF),
            dma((2 * SLOTS + 1,)),
            dma((2 * SLOTS + 1,)),
        ],
        compiler_params=pltpu.CompilerParams(vmem_limit_bytes=63 * 2**20),
        name="hand_on",
    )(forward_out, backward_out, averaged)
    return forward_out[None, None], backward_out[None, None], averaged[None, None]


def solution(mesh):
    in_specs = (
        P("section", "replica", None, None, None),
        P("section", "replica", None, None, None),
        P("section", "replica", None, None, None),
        P("section", "replica", None, None),
        P("section", "replica", None),
        P("section", None, None),
        P("section", None, None),
        P("section", None),
        P("section"),
    )
    out_specs = (
        P("section", "replica", None, None, None),
        P("section", "replica", None, None, None),
        P("section", "replica", None, None),
    )
    return jax.shard_map(body, mesh=mesh, in_specs=in_specs, out_specs=out_specs, check_vma=False)
```
